32 devices in a mesh: groups: 2 (over y), ctx: 16 (over z, x, core).
Axes of the slice: x: 2, y: 2, z: 4, core: 2. Of those that a mesh axis runs over, the one named last changes fastest.
Arguments:
- child_q: bfloat16 [32, 128, 4096], P(('groups', 'ctx')), parts along dimension 0, may hold values from -8 to 8
- child_kv: bfloat16 [32, 128, 2, 512], P(('groups', 'ctx')), parts along dimension 0, may hold values from -12 to 12
- prompt_kv: bfloat16 [128, 2, 512], P(('groups', 'ctx')), parts along dimension 0, may hold values from -12 to 12
- parent_kv: bfloat16 [256, 2, 2, 512], P(('groups', 'ctx')), parts along dimension 0, may hold values from -12 to 12
- fork_list: int32 [32], P('groups'), parts along dimension 0, may hold values from 0 to 1
- owner_map: int32 [4, 16], P('groups'), parts along dimension 0, may hold values from 0 to 15, each once within a row
- lengths: int32 [4], P('groups'), parts along dimension 0, may hold values from 1 to 128, as said below
Outputs:
- child_out: bfloat16 [32, 128, 4096], P(('groups', 'ctx')), parts along dimension 0
The draws below stay inside these ranges and needn't reach their ends.
There are 2 independent parts, one for each index of `groups`. The reference program is written for one: setup_inputs(seed, part) draws one part's arguments, and reference() takes and returns one part's arrays. A program takes and returns all parts, laid end to end along the dimension named above; each array names one. Nothing has to cross between parts.
Inputs may be any that keep to these rules, and one draw needn't show every extreme that they name: `lengths`: some parent has all 128 positions valid.
All inputs are finite; a program needn't handle non-finite values.
Results may differ from the reference program's by a relative error of at most 0.0032.
Values may be sent and summed in bfloat16 or wider, within the bound.
A program may use at most 64 MiB of HBM per device.

```python
import math
import jax
import jax.numpy as jnp
import numpy as np
from jax import lax

HQ = 32
KVH = 4
HD = 128
SPAN = 128
SEGD = 8
CHILDREN = 16
PARENTS = 2
PROMPT = 64
SEG = 128


def kv_field(key, shape, salt):
    field = jnp.clip(2.0 * jax.random.normal(jax.random.fold_in(key, salt), shape, jnp.float32), -12.0, 12.0)
    return field.astype(jnp.bfloat16)


def draw_child_q(key, part):
    shape = (CHILDREN, SPAN, HQ * HD)
    field = jnp.clip(jax.random.normal(jax.random.fold_in(key, 11), shape, jnp.float32), -6.0, 6.0)
    return field.astype(jnp.bfloat16)


def draw_child_kv(key, part):
    return kv_field(key, (CHILDREN, SPAN, 2, KVH * HD), 23)


def draw_prompt_kv(key, part):
    return kv_field(key, (PROMPT, 2, KVH * HD), 29)


def draw_parent_kv(key, part):
    return kv_field(key, (SEG, PARENTS, 2, KVH * HD), 41)


def draw_lengths(key, part):
    base = jax.random.randint(jax.random.fold_in(key, 31), (PARENTS,), 1, SEG + 1)
    chosen = jax.random.randint(jax.random.fold_in(key, 37), (), 0, PARENTS)
    return jnp.where(jnp.arange(PARENTS) == chosen, SEG, base).astype(jnp.int32)


def set_ends(entries, key, least, high):
    place = [jax.random.randint(jax.random.fold_in(key, axis), (), 0, length) for axis, length in enumerate(entries.shape)]
    widest = entries.shape.index(max(entries.shape))
    neighbour = place[:widest] + [(place[widest] + 1) % entries.shape[widest]] + place[widest + 1:]
    return entries.at[tuple(place)].set(least).at[tuple(neighbour)].set(high)


def rank_bounds(amount, lean):
    weights = [(1 << 20) // math.isqrt(standing ** lean) + 1 for standing in range(1, amount + 1)]
    spread = 1 + sum(weights) // (1 << 30)
    return np.cumsum(np.array([max(1, weight // spread) for weight in weights]))


def ranked(key, shape, number_of, slope):
    listing = rank_bounds(number_of, slope)
    ticket = jax.random.randint(jax.random.fold_in(key, 1), shape, 0, int(listing[number_of - 1]))
    grade = jnp.searchsorted(jnp.asarray(listing, jnp.int32), ticket, side="right")
    return jax.random.permutation(jax.random.fold_in(key, 2), number_of)[grade].astype(jnp.int32)


def setup_inputs(seed: int = 0, part: int = 0) -> dict:
    seeds = jax.random.split(jax.random.key(seed), 8)
    part_splits = jax.random.split(jax.random.fold_in(seeds[7], part), 8)
    return {
        "child_q": draw_child_q(jax.random.fold_in(jax.random.fold_in(seeds[7], part), 71), part),
        "child_kv": draw_child_kv(jax.random.fold_in(jax.random.fold_in(seeds[7], part), 71), part),
        "prompt_kv": draw_prompt_kv(jax.random.fold_in(jax.random.fold_in(seeds[7], part), 71), part),
        "parent_kv": draw_parent_kv(jax.random.fold_in(jax.random.fold_in(seeds[7], part), 71), part),
        "fork_list": set_ends(ranked(part_splits[4], (CHILDREN,), PARENTS, 2), jax.random.fold_in(part_splits[4], 3), 0, PARENTS - 1).astype(jnp.int32),
        "owner_map": jax.vmap(lambda own: jax.random.permutation(own, CHILDREN))(jax.random.split(part_splits[5], PARENTS)).reshape((PARENTS, CHILDREN)).astype(jnp.int32),
        "lengths": draw_lengths(jax.random.fold_in(jax.random.fold_in(seeds[7], part), 71), part),
    }


def level_part(queries, key_rows, value_rows, allowed):
    scaling = queries.shape[1] ** -0.5
    scores = jnp.dot(queries.astype(jnp.float32), key_rows.astype(jnp.float32).T, precision=lax.Precision.HIGHEST) * scaling
    if allowed is not None:
        scores = jnp.where(allowed, scores, -jnp.inf)
    highest = jnp.max(scores, axis=1)
    weights = jnp.exp(scores - highest[:, None])
    if allowed is not None:
        weights = jnp.where(allowed, weights, 0.0)
    weights = lax.optimization_barrier(weights.astype(jnp.bfloat16))
    widened = weights.astype(jnp.float32)
    totals = jnp.sum(widened, axis=1)
    weighted = jnp.dot(widened, value_rows.astype(jnp.float32), precision=lax.Precision.HIGHEST)
    return highest, totals, weighted


def merge_levels(former, latter):
    highest = jnp.maximum(former[0], latter[0])
    weight_one = jnp.exp(former[0] - highest)
    weight_two = jnp.exp(latter[0] - highest)
    totals = former[1] * weight_one + latter[1] * weight_two
    weighted = former[2] * weight_one[:, None] + latter[2] * weight_two[:, None]
    return highest, totals, weighted


def reference(child_q, child_kv, prompt_kv, parent_kv, fork_list, owner_map, lengths):
    group_size = HQ // KVH
    places = jnp.arange(CHILDREN, dtype=jnp.int32)
    query_time = jnp.arange(SPAN * group_size, dtype=jnp.int32) // group_size
    causal = jnp.arange(SPAN, dtype=jnp.int32)[None, :] <= query_time[:, None]

    def one_child(child):
        queries = child_q[child]
        own_rows = child_kv[child]
        parent = fork_list[child]
        segment = jnp.take(parent_kv, parent, axis=1)
        owner_row = owner_map[parent]
        matches = owner_row[None, :] == places[:, None]
        pieces = jnp.sum(jnp.where(matches, places[None, :], 0), axis=1)
        positions = (pieces[:, None] * SEGD + jnp.arange(SEGD, dtype=jnp.int32)[None, :]).reshape(SEG)
        allowed = (positions < lengths[parent])[None, :]
        results = []
        for kv_head in range(KVH):
            low = kv_head * HD
            high = low + HD
            head_queries = queries[:, kv_head * group_size * HD:(kv_head + 1) * group_size * HD].reshape(SPAN * group_size, HD)
            prompt_stats = level_part(head_queries, prompt_kv[:, 0, low:high], prompt_kv[:, 1, low:high], None)
            parent_stats = level_part(head_queries, segment[:, 0, low:high], segment[:, 1, low:high], allowed)
            own_stats = level_part(head_queries, own_rows[:, 0, low:high], own_rows[:, 1, low:high], causal)
            merged = merge_levels(merge_levels(prompt_stats, parent_stats), own_stats)
            results.append((merged[2] / merged[1][:, None]).reshape(SPAN, group_size * HD))
        return jnp.concatenate(results, axis=1).astype(jnp.bfloat16)

    return lax.map(one_child, jnp.arange(CHILDREN, dtype=jnp.int32))
```

```python
import functools
import math

import jax
import jax.numpy as jnp
from jax import lax
from jax.experimental import pallas as pl
from jax.experimental.pallas import tpu as pltpu
from jax.sharding import PartitionSpec as P

KVH = 4
HD = 128
MESH = pl.DeviceIdType.MESH
CORES = 2
COLS = 2
NEG = -1e30
HEADS_PER_BLOCK = 4
GATHER_LIMIT = 4 * 1024 * 1024


def head_rows(queries, kv_head, group_size, head_dim):
    row_count = queries.shape[0]
    column_block = queries[
        :, kv_head * group_size * head_dim : (kv_head + 1) * group_size * head_dim
    ]
    return column_block.reshape(row_count * group_size, head_dim)


def level_part(queries, key_rows, value_rows, allowed):
    scaling = queries.shape[1] ** (-0.5)
    scores = (
        jnp.einsum("qd,kd->qk", queries, key_rows, preferred_element_type=jnp.float32) * scaling
    )
    if allowed is not None:
        scores = jnp.where(allowed, scores, -jnp.inf)
    highest = jnp.max(scores, axis=1)
    weights = jnp.exp(scores - highest[:, None])
    if allowed is not None:
        weights = jnp.where(allowed, weights, 0.0)
    weights = lax.optimization_barrier(weights.astype(jnp.bfloat16))
    totals = jnp.sum(weights.astype(jnp.float32), axis=1)
    weighted = jnp.dot(weights, value_rows, preferred_element_type=jnp.float32)
    return (highest, totals, weighted)


def merge_levels(former, latter):
    highest = jnp.maximum(former[0], latter[0])
    weight_one = jnp.exp(former[0] - highest)
    weight_two = jnp.exp(latter[0] - highest)
    totals = former[1] * weight_one + latter[1] * weight_two
    weighted = former[2] * weight_one[:, None] + latter[2] * weight_two[:, None]
    return (highest, totals, weighted)


def body(child_q, child_kv, prompt_kv, parent_kv, fork_list, owner_map, lengths):
    queries = child_q[0]
    own_rows = child_kv[0]
    span_rows = queries.shape[0]
    kv_width = own_rows.shape[2]
    head_dim = HD
    kv_heads = KVH
    group_size = queries.shape[1] // kv_width
    query_rows = span_rows * group_size
    device = lax.axis_index("ctx")
    axis_size = lax.axis_size("ctx")
    seg_rows = parent_kv.shape[0]
    parent = lax.dynamic_index_in_dim(fork_list, device, 0, keepdims=False)
    owner_row = lax.dynamic_index_in_dim(owner_map, parent, 0, keepdims=False)
    places = jnp.arange(axis_size, dtype=jnp.int32)
    matches = owner_row[None, :] == places[:, None]
    pieces = jnp.sum(jnp.where(matches, places[None, :], 0), axis=1)
    positions = jnp.arange(seg_rows, dtype=jnp.int32)[:, None] + pieces[None, :] * seg_rows
    live_length = lax.dynamic_index_in_dim(lengths, parent, 0, keepdims=False)
    allowed = (positions < live_length).reshape(1, seg_rows * axis_size)
    outgoing = jnp.take(parent_kv, fork_list, axis=1)
    query_time = jnp.arange(query_rows, dtype=jnp.int32) // group_size
    causal = jnp.arange(span_rows, dtype=jnp.int32)[None, :] <= query_time[:, None]
    head_queries = []
    for kv_head in range(kv_heads):
        head_queries.append(head_rows(queries, kv_head, group_size, head_dim))
    prompt_copies = jnp.broadcast_to(
        prompt_kv[:, None], (prompt_kv.shape[0], axis_size, 2, kv_width)
    )
    prompt_in, arrived = (
        lax.all_to_all(prompt_copies, "ctx", split_axis=1, concat_axis=1, tiled=True),
        lax.all_to_all(outgoing, "ctx", split_axis=1, concat_axis=1, tiled=True),
    )
    prompt_all = prompt_in.reshape(prompt_kv.shape[0] * axis_size, 2, kv_width)
    segment = arrived.reshape(seg_rows * axis_size, 2, kv_width)
    results = []
    for kv_head in range(kv_heads):
        low = kv_head * head_dim
        prompt_stats = level_part(
            head_queries[kv_head],
            prompt_all[:, 0, low : low + head_dim],
            prompt_all[:, 1, low : low + head_dim],
            None,
        )
        parent_stats = level_part(
            head_queries[kv_head],
            segment[:, 0, low : low + head_dim],
            segment[:, 1, low : low + head_dim],
            allowed,
        )
        own_stats = level_part(
            head_queries[kv_head],
            own_rows[:, 0, low : low + head_dim],
            own_rows[:, 1, low : low + head_dim],
            causal,
        )
        merged = merge_levels(merge_levels(prompt_stats, parent_stats), own_stats)
        results.append((merged[2] / merged[1][:, None]).reshape(span_rows, group_size * head_dim))
    return jnp.concatenate(results, axis=1).astype(jnp.bfloat16)[None]


def cascade_kernel(
    axis_size,
    q_hbm,
    kv_hbm,
    prompt_hbm,
    parent_hbm,
    fork_hbm,
    owner_hbm,
    length_hbm,
    out_hbm,
    q_ref,
    kv_ref,
    pool,
    acc_ref,
    top_ref,
    out_ref,
    fork_ref,
    owner_ref,
    length_ref,
    local_sem,
    send_sem,
    recv_sem,
    out_sem,
):
    me = lax.axis_index("ctx")
    rows_z = axis_size // (CORES * COLS)
    core = lax.rem(me, CORES)
    col = lax.rem(me // CORES, COLS)
    z = me // (CORES * COLS)
    sibling = me + 1 - 2 * core
    across = me + CORES - 2 * CORES * col
    stride = CORES * COLS

    def place(zz, xx, cc):
        return (zz * COLS + xx) * CORES + cc

    z_peers = [place(lax.rem(z + d, rows_z), col, core) for d in range(1, rows_z)]
    peers = z_peers + [across, sibling]

    barrier = pltpu.get_barrier_semaphore()
    for peer in peers:
        pl.semaphore_signal(barrier, inc=1, device_id={"ctx": peer}, device_id_type=MESH)

    prompt_rows = prompt_hbm.shape[0]
    seg_rows, parents = parent_hbm.shape[:2]
    staging = [pltpu.make_async_copy(prompt_hbm, pool.at[me, pl.ds(0, prompt_rows)], local_sem.at[0])]
    for p in range(parents):
        staging.append(
            pltpu.make_async_copy(
                parent_hbm.at[:, p],
                pool.at[me, pl.ds(prompt_rows + p * seg_rows, seg_rows)],
                local_sem.at[1 + p],
            )
        )
    loads = [
        pltpu.make_async_copy(src, dst, local_sem.at[1 + parents + i])
        for i, (src, dst) in enumerate(
            [
                (kv_hbm.at[0], kv_ref),
                (q_hbm.at[0], q_ref),
                (fork_hbm, fork_ref),
                (owner_hbm, owner_ref),
                (length_hbm, length_ref),
            ]
        )
    ]
    for copy in staging + loads:
        copy.start()
    for copy in staging:
        copy.wait()
    pl.semaphore_wait(barrier, len(peers))

    sends = []

    def send(slot, target):
        copy = pltpu.make_async_remote_copy(
            src_ref=pool.at[slot],
            dst_ref=pool.at[slot],
            send_sem=send_sem.at[len(sends)],
            recv_sem=recv_sem.at[slot],
            device_id={"ctx": target},
            device_id_type=MESH,
        )
        copy.start()
        sends.append(copy)

    def arrive(slot):
        pltpu.make_async_remote_copy(
            src_ref=pool.at[slot],
            dst_ref=pool.at[slot],
            send_sem=send_sem.at[0],
            recv_sem=recv_sem.at[slot],
            device_id={"ctx": sibling},
            device_id_type=MESH,
        ).wait_recv()

    for peer in [across] + z_peers + [sibling]:
        send(me, peer)

    span, width = q_ref.shape
    kv_width = kv_ref.shape[2]
    group = width // kv_width
    rate = math.log2(math.e) / math.sqrt(HD)
    block = min(HEADS_PER_BLOCK, group)
    block_rows = block * span

    def block_queries(first):
        return jnp.concatenate(
            [q_ref[:, (first + i) * HD : (first + i + 1) * HD] for i in range(block)], axis=0
        )

    def scored(queries, keys):
        return lax.dot_general(
            queries, keys, (((1,), (1,)), ((), ())), preferred_element_type=jnp.float32
        )

    def with_ones(values):
        return jnp.concatenate([values, jnp.ones_like(values)], axis=1)

    for copy in loads[:2]:
        copy.wait()
    row_time = lax.rem(lax.broadcasted_iota(jnp.int32, (block_rows, span), 0), span)
    causal = lax.broadcasted_iota(jnp.int32, (block_rows, span), 1) <= row_time

    def own_level(kv_head):
        low = kv_head * HD
        keys = kv_ref[:, 0, low : low + HD]
        values = with_ones(kv_ref[:, 1, low : low + HD])
        for first in range(kv_head * group, (kv_head + 1) * group, block):
            rows = slice(first * span, first * span + block_rows)
            scores = jnp.where(causal, scored(block_queries(first), keys), NEG)
            highest = jnp.max(scores, axis=1, keepdims=True)
            weights = jnp.exp2((scores - highest) * rate).astype(jnp.bfloat16)
            acc_ref[rows, :] = jnp.dot(weights, values, preferred_element_type=jnp.float32)
            top_ref[rows, :] = jnp.broadcast_to(highest, (block_rows, HD))

    kv_heads = kv_width // HD
    half = kv_heads // 2
    for kv_head in range(half):
        own_level(kv_head)
    for d, peer in enumerate(z_peers):
        arrive(peer)
        send(peer, across)
        send(peer, sibling)
    for kv_head in range(half, kv_heads):
        own_level(kv_head)
    far = [place(lax.rem(z + d, rows_z), 1 - col, core) for d in range(rows_z)]
    for slot in far:
        arrive(slot)
        send(slot, sibling)

    for copy in loads[2:]:
        copy.wait()
    parent = fork_ref[me]
    live = length_ref[parent]
    stored = axis_size * seg_rows
    lane = lax.broadcasted_iota(jnp.int32, (1, stored), 1)
    owner_lane, within = lane // seg_rows, lax.rem(lane, seg_rows)
    position = jnp.zeros((1, stored), jnp.int32)
    for j in range(axis_size):
        position = jnp.where(owner_lane == owner_ref[parent, j], j * seg_rows + within, position)
    prompt_all = axis_size * prompt_rows
    bias = jnp.concatenate(
        [jnp.where(position < live, 0.0, NEG), jnp.zeros((1, prompt_all), jnp.float32)], axis=1
    )

    for d in range(rows_z):
        for xx in (col, 1 - col):
            arrive(place(lax.rem(z + d, rows_z), xx, 1 - core))

    start = prompt_rows + parent * seg_rows

    def gathered(index, low):
        segment = pool[:, pl.ds(start, seg_rows), index, low : low + HD].reshape(stored, HD)
        prompt = pool[:, :prompt_rows, index, low : low + HD].reshape(prompt_all, HD)
        return jnp.concatenate([segment, prompt], axis=0)

    writes = []
    for kv_head in range(kv_heads):
        low = kv_head * HD
        keys = gathered(0, low)
        values = with_ones(gathered(1, low))
        for first in range(kv_head * group, (kv_head + 1) * group, block):
            rows = slice(first * span, first * span + block_rows)
            scores = scored(block_queries(first), keys) + bias
            own_top = top_ref[rows, :]
            highest = jnp.maximum(jnp.max(scores, axis=1, keepdims=True), own_top[:, :1])
            weights = jnp.exp2((scores - highest) * rate).astype(jnp.bfloat16)
            part = jnp.dot(weights, values, preferred_element_type=jnp.float32)
            own_weight = jnp.exp2((own_top - highest) * rate)
            weighted = acc_ref[rows, :HD] * own_weight + part[:, :HD]
            totals = acc_ref[rows, HD:] * own_weight + part[:, HD:]
            result = (weighted / totals).astype(jnp.bfloat16)
            for i in range(block):
                out_ref[:, (first + i) * HD : (first + i + 1) * HD] = result[i * span : (i + 1) * span]
        cols = pl.ds(kv_head * group * HD, group * HD)
        write = pltpu.make_async_copy(out_ref.at[:, cols], out_hbm.at[0, :, cols], out_sem.at[kv_head])
        write.start()
        writes.append(write)
    for copy in sends:
        copy.wait_send()
    for write in writes:
        write.wait()


def cascade(child_q, child_kv, prompt_kv, parent_kv, fork_list, owner_map, lengths):
    axis_size = lax.axis_size("ctx")
    span, width = child_q.shape[1:]
    kv_width = child_kv.shape[3]
    piece = prompt_kv.shape[0] + parent_kv.shape[0] * parent_kv.shape[1]
    query_rows = span * (width // HD)
    anywhere = pl.BlockSpec(memory_space=pl.ANY)
    return pl.pallas_call(
        functools.partial(cascade_kernel, axis_size),
        out_shape=jax.ShapeDtypeStruct(child_q.shape, jnp.bfloat16),
        in_specs=[anywhere] * 7,
        out_specs=anywhere,
        scratch_shapes=[
            pltpu.VMEM((span, width), jnp.bfloat16),
            pltpu.VMEM((span, 2, kv_width), jnp.bfloat16),
            pltpu.VMEM((axis_size, piece, 2, kv_width), jnp.bfloat16),
            pltpu.VMEM((query_rows, 2 * HD), jnp.float32),
            pltpu.VMEM((query_rows, HD), jnp.float32),
            pltpu.VMEM((span, width), jnp.bfloat16),
            pltpu.SMEM(fork_list.shape, jnp.int32),
            pltpu.SMEM(owner_map.shape, jnp.int32),
            pltpu.SMEM(lengths.shape, jnp.int32),
            pltpu.SemaphoreType.DMA((6 + parent_kv.shape[1],)),
            pltpu.SemaphoreType.DMA((axis_size - 1,)),
            pltpu.SemaphoreType.DMA((axis_size,)),
            pltpu.SemaphoreType.DMA((kv_width // HD,)),
        ],
        compiler_params=pltpu.CompilerParams(
            collective_id=0, has_side_effects=True, vmem_limit_bytes=40 * 1024 * 1024
        ),
    )(child_q, child_kv, prompt_kv, parent_kv, fork_list, owner_map, lengths)


def choose(child_q, child_kv, prompt_kv, parent_kv, fork_list, owner_map, lengths):
    axis_size = lax.axis_size("ctx")
    args = (child_q, child_kv, prompt_kv, parent_kv, fork_list, owner_map, lengths)
    gathered_bytes = 2 * axis_size * (prompt_kv.size + parent_kv.size)
    if gathered_bytes <= GATHER_LIMIT and axis_size % (CORES * COLS) == 0:
        return cascade(*args)
    return body(*args)


def solution(mesh):
    placed = (
        P(("groups", "ctx"), None, None),
        P(("groups", "ctx"), None, None, None),
        P(("groups", "ctx"), None, None),
        P(("groups", "ctx"), None, None, None),
        P("groups"),
        P("groups", None),
        P("groups"),
    )
    return jax.shard_map(
        choose,
        mesh=mesh,
        in_specs=placed,
        out_specs=P(("groups", "ctx"), None, None),
        check_vma=False,
    )
```

```python
import functools
import math

import jax
import jax.numpy as jnp
from jax import lax
from jax.experimental import pallas as pl
from jax.experimental.pallas import tpu as pltpu
from jax.sharding import PartitionSpec as P

KVH = 4
HD = 128
MESH = pl.DeviceIdType.MESH
CORES = 2
COLS = 2
NEG = -1e30
HEADS_PER_BLOCK = 4
GATHER_LIMIT = 4 * 1024 * 1024


def head_rows(queries, kv_head, group_size, head_dim):
    row_count = queries.shape[0]
    column_block = queries[
        :, kv_head * group_size * head_dim : (kv_head + 1) * group_size * head_dim
    ]
    return column_block.reshape(row_count * group_size, head_dim)


def level_part(queries, key_rows, value_rows, allowed):
    scaling = queries.shape[1] ** (-0.5)
    scores = (
        jnp.einsum("qd,kd->qk", queries, key_rows, preferred_element_type=jnp.float32) * scaling
    )
    if allowed is not None:
        scores = jnp.where(allowed, scores, -jnp.inf)
    highest = jnp.max(scores, axis=1)
    weights = jnp.exp(scores - highest[:, None])
    if allowed is not None:
        weights = jnp.where(allowed, weights, 0.0)
    weights = lax.optimization_barrier(weights.astype(jnp.bfloat16))
    totals = jnp.sum(weights.astype(jnp.float32), axis=1)
    weighted = jnp.dot(weights, value_rows, preferred_element_type=jnp.float32)
    return (highest, totals, weighted)


def merge_levels(former, latter):
    highest = jnp.maximum(former[0], latter[0])
    weight_one = jnp.exp(former[0] - highest)
    weight_two = jnp.exp(latter[0] - highest)
    totals = former[1] * weight_one + latter[1] * weight_two
    weighted = former[2] * weight_one[:, None] + latter[2] * weight_two[:, None]
    return (highest, totals, weighted)


def body(child_q, child_kv, prompt_kv, parent_kv, fork_list, owner_map, lengths):
    queries = child_q[0]
    own_rows = child_kv[0]
    span_rows = queries.shape[0]
    kv_width = own_rows.shape[2]
    head_dim = HD
    kv_heads = KVH
    group_size = queries.shape[1] // kv_width
    query_rows = span_rows * group_size
    device = lax.axis_index("ctx")
    axis_size = lax.axis_size("ctx")
    seg_rows = parent_kv.shape[0]
    parent = lax.dynamic_index_in_dim(fork_list, device, 0, keepdims=False)
    owner_row = lax.dynamic_index_in_dim(owner_map, parent, 0, keepdims=False)
    places = jnp.arange(axis_size, dtype=jnp.int32)
    matches = owner_row[None, :] == places[:, None]
    pieces = jnp.sum(jnp.where(matches, places[None, :], 0), axis=1)
    positions = jnp.arange(seg_rows, dtype=jnp.int32)[:, None] + pieces[None, :] * seg_rows
    live_length = lax.dynamic_index_in_dim(lengths, parent, 0, keepdims=False)
    allowed = (positions < live_length).reshape(1, seg_rows * axis_size)
    outgoing = jnp.take(parent_kv, fork_list, axis=1)
    query_time = jnp.arange(query_rows, dtype=jnp.int32) // group_size
    causal = jnp.arange(span_rows, dtype=jnp.int32)[None, :] <= query_time[:, None]
    head_queries = []
    for kv_head in range(kv_heads):
        head_queries.append(head_rows(queries, kv_head, group_size, head_dim))
    prompt_copies = jnp.broadcast_to(
        prompt_kv[:, None], (prompt_kv.shape[0], axis_size, 2, kv_width)
    )
    prompt_in, arrived = (
        lax.all_to_all(prompt_copies, "ctx", split_axis=1, concat_axis=1, tiled=True),
        lax.all_to_all(outgoing, "ctx", split_axis=1, concat_axis=1, tiled=True),
    )
    prompt_all = prompt_in.reshape(prompt_kv.shape[0] * axis_size, 2, kv_width)
    segment = arrived.reshape(seg_rows * axis_size, 2, kv_width)
    results = []
    for kv_head in range(kv_heads):
        low = kv_head * head_dim
        prompt_stats = level_part(
            head_queries[kv_head],
            prompt_all[:, 0, low : low + head_dim],
            prompt_all[:, 1, low : low + head_dim],
            None,
        )
        parent_stats = level_part(
            head_queries[kv_head],
            segment[:, 0, low : low + head_dim],
            segment[:, 1, low : low + head_dim],
            allowed,
        )
        own_stats = level_part(
            head_queries[kv_head],
            own_rows[:, 0, low : low + head_dim],
            own_rows[:, 1, low : low + head_dim],
            causal,
        )
        merged = merge_levels(merge_levels(prompt_stats, parent_stats), own_stats)
        results.append((merged[2] / merged[1][:, None]).reshape(span_rows, group_size * head_dim))
    return jnp.concatenate(results, axis=1).astype(jnp.bfloat16)[None]


def cascade_kernel(
    axis_size,
    q_hbm,
    kv_hbm,
    prompt_hbm,
    parent_hbm,
    fork_hbm,
    owner_hbm,
    length_hbm,
    out_hbm,
    q_ref,
    kv_ref,
    pool,
    acc_ref,
    top_ref,
    out_ref,
    fork_ref,
    owner_ref,
    length_ref,
    local_sem,
    send_sem,
    recv_sem,
    out_sem,
):
    me = lax.axis_index("ctx")
    rows_z = axis_size // (CORES * COLS)
    core = lax.rem(me, CORES)
    col = lax.rem(me // CORES, COLS)
    z = me // (CORES * COLS)
    sibling = me + 1 - 2 * core
    across = me + CORES - 2 * CORES * col
    stride = CORES * COLS

    def place(zz, xx, cc):
        return (zz * COLS + xx) * CORES + cc

    z_peers = [place(lax.rem(z + d, rows_z), col, core) for d in range(1, rows_z)]
    peers = z_peers + [across, sibling]

    barrier = pltpu.get_barrier_semaphore()
    for peer in peers:
        pl.semaphore_signal(barrier, inc=1, device_id={"ctx": peer}, device_id_type=MESH)

    prompt_rows = prompt_hbm.shape[0]
    seg_rows, parents = parent_hbm.shape[:2]
    staging = [pltpu.make_async_copy(prompt_hbm, pool.at[me, pl.ds(0, prompt_rows)], local_sem.at[0])]
    for p in range(parents):
        staging.append(
            pltpu.make_async_copy(
                parent_hbm.at[:, p],
                pool.at[me, pl.ds(prompt_rows + p * seg_rows, seg_rows)],
                local_sem.at[1 + p],
            )
        )
    loads = [
        pltpu.make_async_copy(src, dst, local_sem.at[1 + parents + i])
        for i, (src, dst) in enumerate(
            [
                (kv_hbm.at[0], kv_ref),
                (q_hbm.at[0], q_ref),
                (fork_hbm, fork_ref),
                (owner_hbm, owner_ref),
                (length_hbm, length_ref),
            ]
        )
    ]
    for copy in staging + loads:
        copy.start()
    for copy in staging:
        copy.wait()
    pl.semaphore_wait(barrier, len(peers))

    sends = []

    def send(slot, target):
        copy = pltpu.make_async_remote_copy(
            src_ref=pool.at[slot],
            dst_ref=pool.at[slot],
            send_sem=send_sem.at[len(sends)],
            recv_sem=recv_sem.at[slot],
            device_id={"ctx": target},
            device_id_type=MESH,
        )
        copy.start()
        sends.append(copy)

    def arrive(slot):
        pltpu.make_async_remote_copy(
            src_ref=pool.at[slot],
            dst_ref=pool.at[slot],
            send_sem=send_sem.at[0],
            recv_sem=recv_sem.at[slot],
            device_id={"ctx": sibling},
            device_id_type=MESH,
        ).wait_recv()

    for peer in [across] + z_peers + [sibling]:
        send(me, peer)

    span, width = q_ref.shape
    kv_width = kv_ref.shape[2]
    group = width // kv_width
    rate = math.log2(math.e) / math.sqrt(HD)
    block = min(HEADS_PER_BLOCK, group)
    block_rows = block * span

    def block_queries(first):
        return jnp.concatenate(
            [q_ref[:, (first + i) * HD : (first + i + 1) * HD] for i in range(block)], axis=0
        )

    def scored(queries, keys):
        return lax.dot_general(
            queries, keys, (((1,), (1,)), ((), ())), preferred_element_type=jnp.float32
        )

    def with_ones(values):
        return jnp.concatenate([values, jnp.ones_like(values)], axis=1)

    for copy in loads[:2]:
        copy.wait()
    row_time = lax.rem(lax.broadcasted_iota(jnp.int32, (block_rows, span), 0), span)
    causal = lax.broadcasted_iota(jnp.int32, (block_rows, span), 1) <= row_time

    def own_level(kv_head):
        low = kv_head * HD
        keys = kv_ref[:, 0, low : low + HD]
        values = with_ones(kv_ref[:, 1, low : low + HD])
        for first in range(kv_head * group, (kv_head + 1) * group, block):
            rows = slice(first * span, first * span + block_rows)
            scores = jnp.where(causal, scored(block_queries(first), keys), NEG)
            highest = jnp.max(scores, axis=1, keepdims=True)
            weights = jnp.exp2((scores - highest) * rate).astype(jnp.bfloat16)
            acc_ref[rows, :] = jnp.dot(weights, values, preferred_element_type=jnp.float32)
            top_ref[rows, :] = jnp.broadcast_to(highest, (block_rows, HD))

    kv_heads = kv_width // HD
    half = kv_heads // 2
    for kv_head in range(half):
        own_level(kv_head)
    for d, peer in enumerate(z_peers):
        arrive(peer)
        send(peer, across)
        send(peer, sibling)
    for kv_head in range(half, kv_heads):
        own_level(kv_head)
    far = [place(lax.rem(z + d, rows_z), 1 - col, core) for d in range(rows_z)]
    for slot in far:
        arrive(slot)
        send(slot, sibling)

    for copy in loads[2:]:
        copy.wait()
    parent = fork_ref[me]
    live = length_ref[parent]
    stored = axis_size * seg_rows
    lane = lax.broadcasted_iota(jnp.int32, (1, stored), 1)
    owner_lane, within = lane // seg_rows, lax.rem(lane, seg_rows)
    position = jnp.zeros((1, stored), jnp.int32)
    for j in range(axis_size):
        position = jnp.where(owner_lane == owner_ref[parent, j], j * seg_rows + within, position)
    prompt_all = axis_size * prompt_rows
    bias = jnp.concatenate(
        [jnp.where(position < live, 0.0, NEG), jnp.zeros((1, prompt_all), jnp.float32)], axis=1
    )

    for d in range(rows_z):
        for xx in (col, 1 - col):
            arrive(place(lax.rem(z + d, rows_z), xx, 1 - core))

    start = prompt_rows + parent * seg_rows

    def gathered(index, low):
        segment = pool[:, pl.ds(start, seg_rows), index, low : low + HD].reshape(stored, HD)
        prompt = pool[:, :prompt_rows, index, low : low + HD].reshape(prompt_all, HD)
        return jnp.concatenate([segment, prompt], axis=0)

    writes = []
    for kv_head in range(kv_heads):
        low = kv_head * HD
        keys = gathered(0, low)
        values = with_ones(gathered(1, low))
        for first in range(kv_head * group, (kv_head + 1) * group, block):
            rows = slice(first * span, first * span + block_rows)
            scores = scored(block_queries(first), keys) + bias
            own_top = top_ref[rows, :]
            highest = jnp.maximum(jnp.max(scores, axis=1, keepdims=True), own_top[:, :1])
            weights = jnp.exp2((scores - highest) * rate).astype(jnp.bfloat16)
            part = jnp.dot(weights, values, preferred_element_type=jnp.float32)
            own_weight = jnp.exp2((own_top - highest) * rate)
            weighted = acc_ref[rows, :HD] * own_weight + part[:, :HD]
            totals = acc_ref[rows, HD:] * own_weight + part[:, HD:]
            result = (weighted / totals).astype(jnp.bfloat16)
            for i in range(block):
                out_ref[:, (first + i) * HD : (first + i + 1) * HD] = result[i * span : (i + 1) * span]
        cols = pl.ds(kv_head * group * HD, group * HD)
        write = pltpu.make_async_copy(out_ref.at[:, cols], out_hbm.at[0, :, cols], out_sem.at[kv_head])
        write.start()
        writes.append(write)
    for copy in sends:
        copy.wait_send()
    for write in writes:
        write.wait()


def cascade(child_q, child_kv, prompt_kv, parent_kv, fork_list, owner_map, lengths):
    axis_size = lax.axis_size("ctx")
    span, width = child_q.shape[1:]
    kv_width = child_kv.shape[3]
    piece = prompt_kv.shape[0] + parent_kv.shape[0] * parent_kv.shape[1]
    query_rows = span * (width // HD)
    anywhere = pl.BlockSpec(memory_space=pltpu.HBM)
    return pl.pallas_call(
        functools.partial(cascade_kernel, axis_size),
        out_shape=jax.ShapeDtypeStruct(child_q.shape, jnp.bfloat16),
        in_specs=[anywhere] * 7,
        out_specs=pl.BlockSpec(memory_space=pl.ANY),
        scratch_shapes=[
            pltpu.VMEM((span, width), jnp.bfloat16),
            pltpu.VMEM((span, 2, kv_width), jnp.bfloat16),
            pltpu.VMEM((axis_size, piece, 2, kv_width), jnp.bfloat16),
            pltpu.VMEM((query_rows, 2 * HD), jnp.float32),
            pltpu.VMEM((query_rows, HD), jnp.float32),
            pltpu.VMEM((span, width), jnp.bfloat16),
            pltpu.SMEM(fork_list.shape, jnp.int32),
            pltpu.SMEM(owner_map.shape, jnp.int32),
            pltpu.SMEM(lengths.shape, jnp.int32),
            pltpu.SemaphoreType.DMA((6 + parent_kv.shape[1],)),
            pltpu.SemaphoreType.DMA((axis_size - 1,)),
            pltpu.SemaphoreType.DMA((axis_size,)),
            pltpu.SemaphoreType.DMA((kv_width // HD,)),
        ],
        compiler_params=pltpu.CompilerParams(
            collective_id=0, has_side_effects=True, vmem_limit_bytes=56 * 1024 * 1024
        ),
    )(child_q, child_kv, prompt_kv, parent_kv, fork_list, owner_map, lengths)


def choose(child_q, child_kv, prompt_kv, parent_kv, fork_list, owner_map, lengths):
    axis_size = lax.axis_size("ctx")
    args = (child_q, child_kv, prompt_kv, parent_kv, fork_list, owner_map, lengths)
    gathered_bytes = 2 * axis_size * (prompt_kv.size + parent_kv.size)
    if gathered_bytes <= GATHER_LIMIT and axis_size % (CORES * COLS) == 0:
        return cascade(*args)
    return body(*args)


def solution(mesh):
    placed = (
        P(("groups", "ctx"), None, None),
        P(("groups", "ctx"), None, None, None),
        P(("groups", "ctx"), None, None),
        P(("groups", "ctx"), None, None, None),
        P("groups"),
        P("groups", None),
        P("groups"),
    )
    return jax.shard_map(
        choose,
        mesh=mesh,
        in_specs=placed,
        out_specs=P(("groups", "ctx"), None, None),
        check_vma=False,
    )
```

```python
import functools
import math

import jax
import jax.numpy as jnp
from jax import lax
from jax.experimental import pallas as pl
from jax.experimental.pallas import tpu as pltpu
from jax.sharding import PartitionSpec as P

KVH = 4
HD = 128
MESH = pl.DeviceIdType.MESH
CORES = 2
COLS = 2
NEG = -1e30
HEADS_PER_BLOCK = 4
GATHER_LIMIT = 4 * 1024 * 1024


def head_rows(queries, kv_head, group_size, head_dim):
    row_count = queries.shape[0]
    column_block = queries[
        :, kv_head * group_size * head_dim : (kv_head + 1) * group_size * head_dim
    ]
    return column_block.reshape(row_count * group_size, head_dim)


def level_part(queries, key_rows, value_rows, allowed):
    scaling = queries.shape[1] ** (-0.5)
    scores = (
        jnp.einsum("qd,kd->qk", queries, key_rows, preferred_element_type=jnp.float32) * scaling
    )
    if allowed is not None:
        scores = jnp.where(allowed, scores, -jnp.inf)
    highest = jnp.max(scores, axis=1)
    weights = jnp.exp(scores - highest[:, None])
    if allowed is not None:
        weights = jnp.where(allowed, weights, 0.0)
    weights = lax.optimization_barrier(weights.astype(jnp.bfloat16))
    totals = jnp.sum(weights.astype(jnp.float32), axis=1)
    weighted = jnp.dot(weights, value_rows, preferred_element_type=jnp.float32)
    return (highest, totals, weighted)


def merge_levels(former, latter):
    highest = jnp.maximum(former[0], latter[0])
    weight_one = jnp.exp(former[0] - highest)
    weight_two = jnp.exp(latter[0] - highest)
    totals = former[1] * weight_one + latter[1] * weight_two
    weighted = former[2] * weight_one[:, None] + latter[2] * weight_two[:, None]
    return (highest, totals, weighted)


def body(child_q, child_kv, prompt_kv, parent_kv, fork_list, owner_map, lengths):
    queries = child_q[0]
    own_rows = child_kv[0]
    span_rows = queries.shape[0]
    kv_width = own_rows.shape[2]
    head_dim = HD
    kv_heads = KVH
    group_size = queries.shape[1] // kv_width
    query_rows = span_rows * group_size
    device = lax.axis_index("ctx")
    axis_size = lax.axis_size("ctx")
    seg_rows = parent_kv.shape[0]
    parent = lax.dynamic_index_in_dim(fork_list, device, 0, keepdims=False)
    owner_row = lax.dynamic_index_in_dim(owner_map, parent, 0, keepdims=False)
    places = jnp.arange(axis_size, dtype=jnp.int32)
    matches = owner_row[None, :] == places[:, None]
    pieces = jnp.sum(jnp.where(matches, places[None, :], 0), axis=1)
    positions = jnp.arange(seg_rows, dtype=jnp.int32)[:, None] + pieces[None, :] * seg_rows
    live_length = lax.dynamic_index_in_dim(lengths, parent, 0, keepdims=False)
    allowed = (positions < live_length).reshape(1, seg_rows * axis_size)
    outgoing = jnp.take(parent_kv, fork_list, axis=1)
    query_time = jnp.arange(query_rows, dtype=jnp.int32) // group_size
    causal = jnp.arange(span_rows, dtype=jnp.int32)[None, :] <= query_time[:, None]
    head_queries = []
    for kv_head in range(kv_heads):
        head_queries.append(head_rows(queries, kv_head, group_size, head_dim))
    prompt_copies = jnp.broadcast_to(
        prompt_kv[:, None], (prompt_kv.shape[0], axis_size, 2, kv_width)
    )
    prompt_in, arrived = (
        lax.all_to_all(prompt_copies, "ctx", split_axis=1, concat_axis=1, tiled=True),
        lax.all_to_all(outgoing, "ctx", split_axis=1, concat_axis=1, tiled=True),
    )
    prompt_all = prompt_in.reshape(prompt_kv.shape[0] * axis_size, 2, kv_width)
    segment = arrived.reshape(seg_rows * axis_size, 2, kv_width)
    results = []
    for kv_head in range(kv_heads):
        low = kv_head * head_dim
        prompt_stats = level_part(
            head_queries[kv_head],
            prompt_all[:, 0, low : low + head_dim],
            prompt_all[:, 1, low : low + head_dim],
            None,
        )
        parent_stats = level_part(
            head_queries[kv_head],
            segment[:, 0, low : low + head_dim],
            segment[:, 1, low : low + head_dim],
            allowed,
        )
        own_stats = level_part(
            head_queries[kv_head],
            own_rows[:, 0, low : low + head_dim],
            own_rows[:, 1, low : low + head_dim],
            causal,
        )
        merged = merge_levels(merge_levels(prompt_stats, parent_stats), own_stats)
        results.append((merged[2] / merged[1][:, None]).reshape(span_rows, group_size * head_dim))
    return jnp.concatenate(results, axis=1).astype(jnp.bfloat16)[None]


def cascade_kernel(
    axis_size,
    q_hbm,
    kv_hbm,
    prompt_hbm,
    parent_hbm,
    fork_hbm,
    owner_hbm,
    length_hbm,
    out_ref,
    q_ref,
    kv_ref,
    near,
    far,
    acc_ref,
    top_ref,
    fork_ref,
    owner_ref,
    length_ref,
    local_sem,
    send_sem,
    recv_sem,
):
    me = lax.axis_index("ctx")
    rows_z = axis_size // (CORES * COLS)
    core = lax.rem(me, CORES)
    col = lax.rem(me // CORES, COLS)
    z = me // (CORES * COLS)
    sibling = me + 1 - 2 * core
    across = me + CORES - 2 * CORES * col
    stride = CORES * COLS

    def place(zz, xx, cc):
        return (zz * COLS + xx) * CORES + cc

    z_peers = [place(lax.rem(z + d, rows_z), col, core) for d in range(1, rows_z)]
    peers = z_peers + [across, sibling]

    barrier = pltpu.get_barrier_semaphore()
    for peer in peers:
        pl.semaphore_signal(barrier, inc=1, device_id={"ctx": peer}, device_id_type=MESH)

    prompt_rows = prompt_hbm.shape[0]
    seg_rows, parents = parent_hbm.shape[:2]
    staging = [pltpu.make_async_copy(prompt_hbm, near.at[me // CORES, pl.ds(0, prompt_rows)], local_sem.at[0])]
    for p in range(parents):
        staging.append(
            pltpu.make_async_copy(
                parent_hbm.at[:, p],
                near.at[me // CORES, pl.ds(prompt_rows + p * seg_rows, seg_rows)],
                local_sem.at[1 + p],
            )
        )
    loads = [
        pltpu.make_async_copy(src, dst, local_sem.at[1 + parents + i])
        for i, (src, dst) in enumerate(
            [
                (kv_hbm.at[0], kv_ref),
                (q_hbm.at[0], q_ref),
                (fork_hbm, fork_ref),
                (owner_hbm, owner_ref),
                (length_hbm, length_ref),
            ]
        )
    ]
    for copy in staging + loads:
        copy.start()
    for copy in staging:
        copy.wait()
    pl.semaphore_wait(barrier, len(peers))

    sends = []

    def hop(slot, target, into, index):
        return pltpu.make_async_remote_copy(
            src_ref=near.at[slot // CORES],
            dst_ref=into.at[slot // CORES],
            send_sem=send_sem.at[index],
            recv_sem=recv_sem.at[slot],
            device_id={"ctx": target},
            device_id_type=MESH,
        )

    def send(slot, target, into):
        copy = hop(slot, target, into, len(sends))
        copy.start()
        sends.append(copy)

    def arrive(slot, into):
        hop(slot, sibling, into, 0).wait_recv()

    for peer in [across] + z_peers:
        send(me, peer, near)
    send(me, sibling, far)

    span, width = q_ref.shape
    kv_width = kv_ref.shape[2]
    group = width // kv_width
    rate = math.log2(math.e) / math.sqrt(HD)
    block = min(HEADS_PER_BLOCK, group)
    block_rows = block * span

    def block_queries(first):
        return jnp.concatenate(
            [q_ref[:, (first + i) * HD : (first + i + 1) * HD] for i in range(block)], axis=0
        )

    def scored(queries, keys):
        return lax.dot_general(
            queries, keys, (((1,), (1,)), ((), ())), preferred_element_type=jnp.float32
        )

    def with_ones(values):
        return jnp.concatenate([values, jnp.ones_like(values)], axis=1)

    for copy in loads[:2]:
        copy.wait()
    row_time = lax.rem(lax.broadcasted_iota(jnp.int32, (block_rows, span), 0), span)
    causal = lax.broadcasted_iota(jnp.int32, (block_rows, span), 1) <= row_time

    def own_level(kv_head):
        low = kv_head * HD
        keys = kv_ref[:, 0, low : low + HD]
        values = with_ones(kv_ref[:, 1, low : low + HD])
        for first in range(kv_head * group, (kv_head + 1) * group, block):
            rows = slice(first * span, first * span + block_rows)
            scores = jnp.where(causal, scored(block_queries(first), keys), NEG)
            highest = jnp.max(scores, axis=1, keepdims=True)
            weights = jnp.exp2((scores - highest) * rate).astype(jnp.bfloat16)
            acc_ref[rows, :] = jnp.dot(weights, values, preferred_element_type=jnp.float32)
            top_ref[rows, :] = jnp.broadcast_to(highest, (block_rows, HD))

    kv_heads = kv_width // HD
    half = kv_heads // 2
    for kv_head in range(half):
        own_level(kv_head)
    for d, peer in enumerate(z_peers):
        arrive(peer, near)
        send(peer, across, near)
        send(peer, sibling, far)
    for kv_head in range(half, kv_heads):
        own_level(kv_head)
    across_slots = [place(lax.rem(z + d, rows_z), 1 - col, core) for d in range(rows_z)]
    for slot in across_slots:
        arrive(slot, near)
        send(slot, sibling, far)

    for copy in loads[2:]:
        copy.wait()
    parent = fork_ref[me]
    live = length_ref[parent]
    pairs = axis_size // CORES
    stored, prompt_half = pairs * seg_rows, pairs * prompt_rows
    lane = lax.broadcasted_iota(jnp.int32, (1, stored), 1)
    owner_lane, within = (lane // seg_rows) * CORES, lax.rem(lane, seg_rows)
    start = prompt_rows + parent * seg_rows

    def bias_of(side):
        position = jnp.zeros((1, stored), jnp.int32)
        for j in range(axis_size):
            owned = owner_lane + side == owner_ref[parent, j]
            position = jnp.where(owned, j * seg_rows + within, position)
        return jnp.concatenate(
            [jnp.where(position < live, 0.0, NEG), jnp.zeros((1, prompt_half), jnp.float32)], axis=1
        )

    def gathered(pool, index, low):
        segment = pool[:, pl.ds(start, seg_rows), index, low : low + HD].reshape(stored, HD)
        prompt = pool[:, :prompt_rows, index, low : low + HD].reshape(prompt_half, HD)
        return jnp.concatenate([segment, prompt], axis=0)

    def gathered_level(pool, bias, last):
        for kv_head in range(kv_heads):
            low = kv_head * HD
            keys = gathered(pool, 0, low)
            values = with_ones(gathered(pool, 1, low))
            for first in range(kv_head * group, (kv_head + 1) * group, block):
                rows = slice(first * span, first * span + block_rows)
                scores = scored(block_queries(first), keys) + bias
                former_top = top_ref[rows, :]
                highest = jnp.maximum(jnp.max(scores, axis=1, keepdims=True), former_top)
                weights = jnp.exp2((scores - highest[:, : scores.shape[1]]) * rate).astype(jnp.bfloat16)
                part = jnp.dot(weights, values, preferred_element_type=jnp.float32)
                former = jnp.exp2((former_top - highest) * rate)
                weighted = acc_ref[rows, :HD] * former + part[:, :HD]
                totals = acc_ref[rows, HD:] * former + part[:, HD:]
                if not last:
                    acc_ref[rows, :HD] = weighted
                    acc_ref[rows, HD:] = totals
                    top_ref[rows, :] = highest
                    continue
                result = (weighted / totals).astype(jnp.bfloat16)
                for i in range(block):
                    cols = slice((first + i) * HD, (first + i + 1) * HD)
                    out_ref[0, :, cols] = result[i * span : (i + 1) * span]

    near_bias, far_bias = bias_of(core), bias_of(1 - core)
    gathered_level(near, near_bias, False)
    for d in range(rows_z):
        for xx in (col, 1 - col):
            arrive(place(lax.rem(z + d, rows_z), xx, 1 - core), far)
    gathered_level(far, far_bias, True)
    for copy in sends:
        copy.wait_send()


def cascade(child_q, child_kv, prompt_kv, parent_kv, fork_list, owner_map, lengths):
    operands = (child_q, child_kv, prompt_kv, parent_kv, fork_list, owner_map, lengths)
    axis_size = lax.axis_size("ctx")
    span, width = child_q.shape[1:]
    kv_width = child_kv.shape[3]
    piece = prompt_kv.shape[0] + parent_kv.shape[0] * parent_kv.shape[1]
    query_rows = span * (width // HD)
    anywhere = pl.BlockSpec(memory_space=pltpu.HBM)
    return pl.pallas_call(
        functools.partial(cascade_kernel, axis_size),
        out_shape=jax.ShapeDtypeStruct(child_q.shape, jnp.bfloat16),
        in_specs=[anywhere] * 7,
        out_specs=pl.BlockSpec(memory_space=pltpu.VMEM),
        scratch_shapes=[
            pltpu.VMEM((span, width), jnp.bfloat16),
            pltpu.VMEM((span, 2, kv_width), jnp.bfloat16),
            pltpu.VMEM((axis_size // CORES, piece, 2, kv_width), jnp.bfloat16),
            pltpu.VMEM((axis_size // CORES, piece, 2, kv_width), jnp.bfloat16),
            pltpu.VMEM((query_rows, 2 * HD), jnp.float32),
            pltpu.VMEM((query_rows, HD), jnp.float32),
            pltpu.SMEM(fork_list.shape, jnp.int32),
            pltpu.SMEM(owner_map.shape, jnp.int32),
            pltpu.SMEM(lengths.shape, jnp.int32),
            pltpu.SemaphoreType.DMA((6 + parent_kv.shape[1],)),
            pltpu.SemaphoreType.DMA((axis_size - 1,)),
            pltpu.SemaphoreType.DMA((axis_size,)),
        ],
        compiler_params=pltpu.CompilerParams(
            collective_id=0, has_side_effects=True, vmem_limit_bytes=40 * 1024 * 1024
        ),
    )(*[pltpu.with_memory_space_constraint(operand, pltpu.HBM) for operand in operands])


def choose(child_q, child_kv, prompt_kv, parent_kv, fork_list, owner_map, lengths):
    axis_size = lax.axis_size("ctx")
    args = (child_q, child_kv, prompt_kv, parent_kv, fork_list, owner_map, lengths)
    gathered_bytes = 2 * axis_size * (prompt_kv.size + parent_kv.size)
    half_keys = axis_size // CORES * (prompt_kv.shape[0] + parent_kv.shape[0])
    if gathered_bytes <= GATHER_LIMIT and axis_size % (CORES * COLS) == 0 and half_keys <= HD:
        return cascade(*args)
    return body(*args)


def solution(mesh):
    placed = (
        P(("groups", "ctx"), None, None),
        P(("groups", "ctx"), None, None, None),
        P(("groups", "ctx"), None, None),
        P(("groups", "ctx"), None, None, None),
        P("groups"),
        P("groups", None),
        P("groups"),
    )
    return jax.shard_map(
        choose,
        mesh=mesh,
        in_specs=placed,
        out_specs=P(("groups", "ctx"), None, None),
        check_vma=False,
    )
```
